256 devices in a mesh: section: 64 (over z_lo, y, x, core), tp: 4 (over z_hi).
Axes of the slice: x: 4, y: 4, z: 8 (z_hi: 4, z_lo: 2; z = z_hi * 2 + z_lo), core: 2. Of those that a mesh axis runs over, the one named last changes fastest.
Arguments:
- kept_rows: bfloat16 [24576, 18432], P('section', 'tp'), may hold values from -8 to 8, as said below
- parked_rows: bfloat16 [16384, 18432], P(('section', 'tp')), may hold values from -8 to 8, as said below
- grad_out: bfloat16 [32768, 6144], P('section', 'tp'), may hold values from -6 to 6
- lengths: int32 [3], replicated, may hold values from 64 to 256, as said below
- evicted: int32 [64], P('section'), may hold values from 0 to 2, as said below
Outputs:
- received: bfloat16 [32768, 18432], P('section', 'tp')
The draws below stay inside these ranges and needn't reach their ends.
Inputs may be any that keep to these rules, and one draw needn't show every extreme that they name: `lengths`: the micro-batches fill the 4 blocks of 128 tokens in order; one spans 2 blocks and is full, each other fits one block. `evicted`: some section parks its micro-batch of 2 blocks and some section parks a micro-batch of one block. `kept_rows`: section i's own rows of the micro-batches it does not park, in buffer order, then unused rows. `parked_rows`: the rows that section i holds for its partner section: that section's parked micro-batch in buffer order, then unused rows.
All inputs are finite; a program needn't handle non-finite values.
Results may differ from the reference program's by a relative error of at most 0.0054.
Values may be sent and summed in bfloat16 or wider, within the bound.
No kernel may reach another device: no remote copies, remote signals or barrier semaphores. Data moves between devices by JAX's collectives and lax.ppermute only.
A program may use at most 128 MiB of HBM per device.

```python
import jax
import jax.numpy as jnp
from jax import lax

HEADS = 48
HD = 128
BLK = 128
MB = 3
NB = 4
PB = 2
KB = 3
TOKENS = 512
N_SECTION = 64


def plan_draw(key):
    key_long, key_short, key_evict = jax.random.split(key, 3)
    long_index = jax.random.randint(key_long, (), 0, MB)
    indices = jnp.arange(MB)
    shorts = jax.random.randint(key_short, (MB,), BLK // 2, BLK + 1)
    lengths = jnp.where(indices == long_index, PB * BLK, shorts).astype(jnp.int32)
    evicted = jax.random.randint(key_evict, (N_SECTION,), 0, MB)
    for section_pos in range(MB):
        evicted = evicted.at[section_pos].set((long_index + section_pos) % MB)
    return (lengths, evicted.astype(jnp.int32))


def draw_lengths(key, part):
    lengths, evicted = plan_draw(key)
    return lengths


def draw_evicted(key, part):
    lengths, evicted = plan_draw(key)
    return evicted


def draw_kept_rows(key, part):
    key = jax.random.fold_in(key, 5)
    full_shape = (N_SECTION, KB * BLK, HEADS, 3, HD)
    values = jax.random.truncated_normal(key, -6.0, 6.0, full_shape, jnp.float32)
    return values.reshape(N_SECTION * KB * BLK, HEADS * 3 * HD).astype(jnp.bfloat16)


def draw_parked_rows(key, part):
    key = jax.random.fold_in(key, 7)
    full_shape = (N_SECTION, PB * BLK, HEADS, 3, HD)
    values = jax.random.truncated_normal(key, -6.0, 6.0, full_shape, jnp.float32)
    return values.reshape(N_SECTION * PB * BLK, HEADS * 3 * HD).astype(jnp.bfloat16)


def levels(rng, dims, cuts, least, high):
    loudness = 1.0
    for dim, parts in cuts:
        heights = jax.random.uniform(jax.random.fold_in(jax.random.fold_in(rng, 6), dim), (parts,), jnp.float32, least / len(cuts), high / len(cuts))
        loudness = loudness * jnp.repeat(jnp.exp(heights), dims[dim] // parts).reshape((-1,) + (1,) * (len(dims) - 1 - dim))
    return loudness


def centred(own_key, extent, width, most, pieces=(), kind=jnp.bfloat16):
    array = width * jax.random.normal(own_key, extent, jnp.float32)
    if pieces:
        array = array * levels(own_key, extent, pieces, -0.22, 0.18)
    return jnp.clip(array, -most, most).astype(kind)


def setup_inputs(seed: int = 0) -> dict:
    splits = jax.random.split(jax.random.key(seed), 6)
    return {
        "kept_rows": draw_kept_rows(jax.random.fold_in(splits[5], 71), 0),
        "parked_rows": draw_parked_rows(jax.random.fold_in(splits[5], 71), 0),
        "grad_out": centred(splits[2], (N_SECTION * TOKENS, HEADS * HD), 1.0, 6.0, ((0, 64), (1, 4))),
        "lengths": draw_lengths(jax.random.fold_in(splits[5], 71), 0),
        "evicted": draw_evicted(jax.random.fold_in(splits[5], 71), 0),
    }


def layout_plan(lengths, evicted):
    counts = ((lengths + BLK - 1) // BLK).astype(jnp.int32)
    block_end = jnp.cumsum(counts).astype(jnp.int32)
    starts = (block_end - counts).astype(jnp.int32)
    blocks = jnp.arange(NB, dtype=jnp.int32)
    segment = jnp.sum((blocks[:, None] >= block_end[None, :]).astype(jnp.int32), axis=1).astype(jnp.int32)
    picked = jnp.arange(MB, dtype=jnp.int32) == evicted
    first_block = jnp.sum(jnp.where(picked, starts, 0)).astype(jnp.int32)
    span_len = jnp.sum(jnp.where(picked, counts, 0)).astype(jnp.int32)
    kept_index = blocks - jnp.where(blocks >= first_block + span_len, span_len, 0)
    source = jnp.where(segment == evicted, KB + blocks - first_block, kept_index).astype(jnp.int32)
    tok_owner = jnp.repeat(segment, BLK, total_repeat_length=NB * BLK)
    row_ids = jnp.arange(NB * BLK, dtype=jnp.int32)
    member = tok_owner[:, None] == jnp.arange(MB, dtype=jnp.int32)[None, :]
    offset = (row_ids - BLK * jnp.sum(jnp.where(member, starts[None, :], 0), axis=1)).astype(jnp.int32)
    inside = offset < jnp.sum(jnp.where(member, lengths[None, :], 0), axis=1)
    return source, tok_owner, offset, inside


def assemble(kept_rows, fetched, source):
    columns = kept_rows.shape[1]
    stacked = jnp.concatenate([kept_rows.reshape(KB, BLK, columns), fetched.reshape(PB, BLK, columns)], axis=0)
    return jnp.take(stacked, source, axis=0).reshape(NB * BLK, columns)


def backward(stash, out_grad, tok_owner, offset, inside):
    tokens = stash.shape[0]
    head_count = stash.shape[1] // (3 * HD)
    split = stash.reshape(tokens, head_count, 3, HD).astype(jnp.float32)
    queries, key_rows, value_rows = split[:, :, 0], split[:, :, 1], split[:, :, 2]
    masked = jnp.where(inside[:, None], out_grad, jnp.zeros((), jnp.bfloat16))
    grad_rows = masked.reshape(tokens, head_count, HD).astype(jnp.float32)
    factor = HD ** -0.5
    scores = jnp.einsum("qhd,khd->hqk", queries, key_rows) * factor
    allowed = (tok_owner[:, None] == tok_owner[None, :]) & (offset[None, :] <= offset[:, None]) & inside[None, :]
    scores = jnp.where(allowed[None], scores, -jnp.inf)
    row_max = jnp.max(scores, axis=-1, keepdims=True)
    raised = jnp.exp(scores - row_max)
    attend = raised / jnp.sum(raised, axis=-1, keepdims=True)
    attend_low = lax.optimization_barrier(attend.astype(jnp.bfloat16)).astype(jnp.float32)
    value_grad = jnp.einsum("hqk,qhd->khd", attend_low, grad_rows).astype(jnp.bfloat16)
    prob_grad = jnp.einsum("qhd,khd->hqk", grad_rows, value_rows)
    row_dot = jnp.sum(attend * prob_grad, axis=-1, keepdims=True)
    score_grad = lax.optimization_barrier((attend * (prob_grad - row_dot)).astype(jnp.bfloat16)).astype(jnp.float32)
    query_grad = (jnp.einsum("hqk,khd->qhd", score_grad, key_rows) * factor).astype(jnp.bfloat16)
    key_grad = (jnp.einsum("hqk,qhd->khd", score_grad, queries) * factor).astype(jnp.bfloat16)
    return jnp.stack([query_grad, key_grad, value_grad], axis=2).reshape(tokens, head_count * 3 * HD)


def reference(kept_rows, parked_rows, grad_out, lengths, evicted):
    columns = HEADS * 3 * HD
    kept_all = kept_rows.reshape(N_SECTION, KB * BLK, columns)
    partnered = jnp.roll(parked_rows.reshape(N_SECTION, PB * BLK, columns), N_SECTION // 2, axis=0)
    grad_all = grad_out.reshape(N_SECTION, TOKENS, HEADS * HD)

    def one_section(section_args):
        kept_one, parked_one, grad_one, section_evict = section_args
        source, tok_owner, offset, inside = layout_plan(lengths, section_evict)
        stash = assemble(kept_one, parked_one, source)
        return backward(stash, grad_one, tok_owner, offset, inside)

    grads = lax.map(one_section, (kept_all, partnered, grad_all, evicted))
    grads = grads.reshape(N_SECTION * TOKENS, columns)
    return jnp.roll(grads, -TOKENS, axis=0)
```

```python
import functools

import jax
import jax.numpy as jnp
from jax import lax
from jax.experimental import pallas as pl
from jax.experimental.pallas import tpu as pltpu
from jax.sharding import PartitionSpec as P

HD = 128
BLK = 128
KB = 3
HW = 3 * HD
FACTOR = HD**-0.5
PER_STEP = 2
HOPS = (3, -3, 1, -1)
KEPT_CHUNKS = (6, 6)
KEPT_COST = 300_000_000
PARKED_COST = 300_000_000
PARKED_CHUNKS = (6, 6)


def pick(index, values):
    return jnp.where(index == 0, values[0], jnp.where(index == 1, values[1], values[2]))


class Plan:
    def __init__(self, lengths, evicted):
        self.lengths = [lengths[m] for m in range(3)]
        counts = [lax.shift_right_logical(n + (BLK - 1), 7) for n in self.lengths]
        self.starts = [jnp.int32(0), counts[0], counts[0] + counts[1]]
        which = evicted[0]
        self.first = pick(which, self.starts)
        self.span = pick(which, counts)
        self.long = self.span > 1

    def segment(self, block):
        return (block >= self.starts[1]).astype(jnp.int32) + (block >= self.starts[2]).astype(jnp.int32)

    def valid(self, block):
        m = self.segment(block)
        return jnp.clip(pick(m, self.lengths) - BLK * (block - pick(m, self.starts)), 0, BLK)

    def kept(self, slot):
        return jnp.minimum(slot + jnp.where(slot >= self.first, self.span, 0), 3)

    def parked(self, slot):
        return jnp.minimum(self.first + slot, 3)

    def late(self, slot):
        return jnp.where(slot == 0, self.first, jnp.where(self.long, self.parked(1), self.kept(2)))


def nt(a, b):
    return lax.dot_general(a, b, (((1,), (1,)), ((), ())), preferred_element_type=jnp.float32)


def nn(a, b):
    return lax.dot_general(a, b, (((1,), (0,)), ((), ())), preferred_element_type=jnp.float32)


def tn(a, b):
    return lax.dot_general(a, b, (((0,), (0,)), ((), ())), preferred_element_type=jnp.float32)


def attention_grads(q, k, v, grads, valids, joins):
    count = len(q)
    key_ids = lax.broadcasted_iota(jnp.int32, (BLK, BLK), 0)
    query_ids = lax.broadcasted_iota(jnp.int32, (BLK, BLK), 1)
    dq, dk, dv = [None] * count, [None] * count, [None] * count
    for j in range(count):
        grad = jnp.where(key_ids < valids[j], grads[j], jnp.zeros((), jnp.bfloat16))
        allowed = (key_ids <= query_ids) & (key_ids < valids[j])
        if j == 0:
            keys, values = k[0], v[0]
        else:
            keys, values = jnp.concatenate([k[j - 1], k[j]]), jnp.concatenate([v[j - 1], v[j]])
            before = jnp.broadcast_to(joins[j], (BLK, BLK))
            allowed = jnp.concatenate([before, allowed])
        scores = jnp.where(allowed, nt(keys, q[j]) * FACTOR, -jnp.inf)
        raised = jnp.exp(scores - jnp.max(scores, axis=0, keepdims=True))
        attend = raised * (1.0 / jnp.sum(raised, axis=0, keepdims=True))
        prob_grad = nt(values, grad)
        row_dot = jnp.sum(attend * prob_grad, axis=0, keepdims=True)
        score_grad = (attend * (prob_grad - row_dot)).astype(jnp.bfloat16)
        value_part = nn(attend.astype(jnp.bfloat16), grad)
        key_part = nn(score_grad, q[j])
        dq[j] = tn(score_grad, keys)
        if j == 0:
            dk[0], dv[0] = key_part, value_part
        else:
            dk[j - 1], dv[j - 1] = dk[j - 1] + key_part[:BLK], dv[j - 1] + value_part[:BLK]
            dk[j], dv[j] = key_part[BLK:], value_part[BLK:]
    low = lambda x: x.astype(jnp.bfloat16)
    return [low(x * FACTOR) for x in dq], [low(x * FACTOR) for x in dk], [low(x) for x in dv]


def worth(flops):
    return pl.CostEstimate(flops=flops, bytes_accessed=1 << 20, transcendentals=0)


def columns(head, part):
    return slice(head * HW + part * HD, head * HW + (part + 1) * HD)


def kept_kernel(lengths, evicted, rows, g0, g1, g2, early, third):
    plan = Plan(lengths, evicted)
    blocks = [plan.kept(j) for j in range(KB)]
    valids = [plan.valid(b) for b in blocks]
    segments = [plan.segment(b) for b in blocks]
    joins = [None] + [(segments[j] == segments[j - 1]) & jnp.logical_not(plan.long) for j in range(1, KB)]
    for head in range(PER_STEP):
        q, k, v = ([rows[j * BLK : (j + 1) * BLK, columns(head, p)] for j in range(KB)] for p in range(3))
        grads = [g[:, head * HD : (head + 1) * HD] for g in (g0, g1, g2)]
        for part, made in enumerate(attention_grads(q, k, v, grads, valids, joins)):
            early[0:BLK, columns(head, part)] = made[0]
            early[BLK : 2 * BLK, columns(head, part)] = made[1]
            third[:, columns(head, part)] = made[2]


def kept_part(lengths, evicted, kept_rows, grad_out, first, heads):
    at = first // PER_STEP
    grad_spec = lambda j: pl.BlockSpec(
        (BLK, PER_STEP * HD), lambda i, ln, ev: (Plan(ln, ev).kept(j), at + i)
    )
    return pl.pallas_call(
        kept_kernel,
        grid_spec=pltpu.PrefetchScalarGridSpec(
            num_scalar_prefetch=2,
            grid=(heads // PER_STEP,),
            in_specs=[pl.BlockSpec((KB * BLK, PER_STEP * HW), lambda i, ln, ev: (0, at + i))]
            + [grad_spec(j) for j in range(KB)],
            out_specs=[
                pl.BlockSpec((2 * BLK, PER_STEP * HW), lambda i, ln, ev: (0, i)),
                pl.BlockSpec((BLK, PER_STEP * HW), lambda i, ln, ev: (0, i)),
            ],
        ),
        out_shape=[
            jax.ShapeDtypeStruct((2 * BLK, heads * HW), jnp.bfloat16),
            jax.ShapeDtypeStruct((BLK, heads * HW), jnp.bfloat16),
        ],
        compiler_params=pltpu.CompilerParams(vmem_limit_bytes=32 << 20),
        cost_estimate=worth(heads * KEPT_COST),
        name="kept_grads",
    )(lengths, evicted, kept_rows, grad_out, grad_out, grad_out)


def parked_kernel(lengths, evicted, quarters, r0, r1, r2, r3, g0, g1, third, late, rows):
    plan = Plan(lengths, evicted)
    quarter = BLK // 2
    for d, piece in enumerate((r0, r1, r2, r3)):
        start = pl.multiple_of(quarters[d] * quarter, quarter)
        rows[pl.ds(start, quarter), :] = piece[...]
    valids = [plan.valid(plan.parked(j)) for j in range(2)]
    joins = [None, plan.long]
    for head in range(PER_STEP):
        q, k, v = ([rows[j * BLK : (j + 1) * BLK, columns(head, p)] for j in range(2)] for p in range(3))
        grads = [g[:, head * HD : (head + 1) * HD] for g in (g0, g1)]
        grads[1] = jnp.where(plan.long, grads[1], jnp.zeros((), jnp.bfloat16))
        for part, made in enumerate(attention_grads(q, k, v, grads, valids, joins)):
            late[0:BLK, columns(head, part)] = made[0]
            late[BLK : 2 * BLK, columns(head, part)] = jnp.where(
                plan.long, made[1], third[:, columns(head, part)]
            )


def parked_part(lengths, evicted, quarters, pieces, grad_out, third, third_at, first, heads):
    at = first // PER_STEP
    third_at = third_at // PER_STEP
    grad_spec = lambda j: pl.BlockSpec(
        (BLK, PER_STEP * HD), lambda i, ln, ev, sh: (Plan(ln, ev).parked(j), at + i)
    )
    return pl.pallas_call(
        parked_kernel,
        grid_spec=pltpu.PrefetchScalarGridSpec(
            num_scalar_prefetch=3,
            grid=(heads // PER_STEP,),
            in_specs=[pl.BlockSpec((BLK // 2, PER_STEP * HW), lambda i, ln, ev, sh: (0, i))] * 4
            + [grad_spec(j) for j in range(2)]
            + [pl.BlockSpec((BLK, PER_STEP * HW), lambda i, ln, ev, sh: (0, third_at + i))],
            out_specs=pl.BlockSpec((2 * BLK, PER_STEP * HW), lambda i, ln, ev, sh: (0, i)),
            scratch_shapes=[pltpu.VMEM((2 * BLK, PER_STEP * HW), jnp.bfloat16)],
        ),
        out_shape=jax.ShapeDtypeStruct((2 * BLK, heads * HW), jnp.bfloat16),
        compiler_params=pltpu.CompilerParams(vmem_limit_bytes=32 << 20),
        cost_estimate=worth(heads * PARKED_COST),
        name="parked_grads",
    )(lengths, evicted, quarters, *pieces, grad_out, grad_out, third)


def place_kernel(slot_of, first, lengths, evicted, piece, *refs):
    out, sems = refs[-2:]
    plan = Plan(lengths, evicted)
    copies = []
    for slot in range(2):
        start = pl.multiple_of(slot_of(plan, slot) * BLK, BLK)
        copies.append(
            pltpu.make_async_copy(
                piece.at[pl.ds(slot * BLK, BLK), :],
                out.at[pl.ds(start, BLK), pl.ds(first * HW, piece.shape[1])],
                sems.at[slot],
            )
        )
    for copy in copies:
        copy.start()
    for copy in copies:
        copy.wait()


def place(lengths, evicted, piece, out, slot_of, first, total):
    base = (lengths, evicted, piece) if out is None else (lengths, evicted, piece, out)
    smem, vmem, hbm = (pl.BlockSpec(memory_space=m) for m in (pltpu.SMEM, pltpu.VMEM, pl.ANY))
    return pl.pallas_call(
        functools.partial(place_kernel, slot_of, first),
        in_specs=[smem, smem, vmem] + [hbm] * (len(base) - 3),
        out_specs=hbm,
        scratch_shapes=[pltpu.SemaphoreType.DMA((2,))],
        out_shape=jax.ShapeDtypeStruct(total, jnp.bfloat16),
        input_output_aliases={} if out is None else {3: 0},
        name="place_rows",
    )(*base)


def shards(kept_rows, parked_rows, grad_out, lengths, evicted):
    sections, peers = lax.axis_size("section"), lax.axis_size("tp")
    half = sections // 2
    ring = 2 * peers
    total = (grad_out.shape[0], kept_rows.shape[1])
    share = total[1]
    spot = 2 * lax.axis_index("tp") + lax.axis_index("section") // half

    def shifted(rows, hops):
        pairs = []
        for s in range(sections):
            for t in range(peers):
                to = (2 * t + s // half + hops) % ring
                pairs.append((s * peers + t, ((s + half) % sections) * peers + to // 2))
        return lax.ppermute(rows, ("section", "tp"), pairs)

    def passed_back(rows):
        return lax.ppermute(rows, "section", [(i, (i - 1) % sections) for i in range(sections)])

    next_evicted = passed_back(evicted)

    arrived = []
    first = 0
    for heads in PARKED_CHUNKS:
        width = heads * HW
        pieces = []
        for hops in HOPS:
            to = lax.rem(spot + hops + ring, ring) // 2
            rows = lax.dynamic_slice(parked_rows, (0, to * share + first * HW), (parked_rows.shape[0], width))
            pieces.append(shifted(rows, hops))
        arrived.append(pieces)
        first += heads
    quarters = jnp.stack([lax.rem(spot - hops + ring, ring) // 2 for hops in HOPS]).astype(jnp.int32)

    out = None
    thirds = []
    received = []
    first = 0

    def after(rows):
        return passed_back(rows)

    for heads in KEPT_CHUNKS:
        early, third = kept_part(lengths, evicted, kept_rows, grad_out, first, heads)
        thirds.append((first, heads, third))
        received.append((after(early), Plan.kept, first))
        first += heads

    first = 0
    for heads, pieces in zip(PARKED_CHUNKS, arrived):
        at, third = next((f, t) for f, n, t in thirds if f <= first and first + heads <= f + n)
        late = parked_part(lengths, evicted, quarters, pieces, grad_out, third, first - at, first, heads)
        received.append((after(late), Plan.late, first))
        first += heads

    for piece, slot_of, first in received:
        out = place(lengths, next_evicted, piece, out, slot_of, first, total)
    return out


def solution(mesh):
    in_specs = (
        P("section", "tp"),
        P(("section", "tp"), None),
        P("section", "tp"),
        P(),
        P("section"),
    )
    out_specs = P("section", "tp")
    return jax.shard_map(shards, mesh=mesh, in_specs=in_specs, out_specs=out_specs, check_vma=False)
```

```python
import functools

import jax
import jax.numpy as jnp
from jax import lax
from jax.experimental import pallas as pl
from jax.experimental.pallas import tpu as pltpu
from jax.sharding import PartitionSpec as P

HD = 128
BLK = 128
KB = 3
HW = 3 * HD
FACTOR = HD**-0.5
FACTOR2 = FACTOR * 1.4426950408889634
KEPT_STEP = 4
PARKED_STEP = 6
VMEM = 56 << 20
HOPS = (3, -3, 1, -1)
KEPT_COST = 1000_000_000
LATE_COST = 4000_000_000
PARKED_COST = 4000_000_000
PARKED_CHUNKS = (6, 6)


def pick(index, values):
    return jnp.where(index == 0, values[0], jnp.where(index == 1, values[1], values[2]))


class Plan:
    def __init__(self, lengths, evicted):
        self.lengths = [lengths[m] for m in range(3)]
        counts = [lax.shift_right_logical(n + (BLK - 1), 7) for n in self.lengths]
        self.starts = [jnp.int32(0), counts[0], counts[0] + counts[1]]
        which = evicted[0]
        self.first = pick(which, self.starts)
        self.span = pick(which, counts)
        self.long = self.span > 1

    def segment(self, block):
        return (block >= self.starts[1]).astype(jnp.int32) + (block >= self.starts[2]).astype(jnp.int32)

    def valid(self, block):
        m = self.segment(block)
        return jnp.clip(pick(m, self.lengths) - BLK * (block - pick(m, self.starts)), 0, BLK)

    def kept(self, slot):
        return jnp.minimum(slot + jnp.where(slot >= self.first, self.span, 0), 3)

    def parked(self, slot):
        return jnp.minimum(self.first + slot, 3)

    def late(self, slot):
        return jnp.where(slot == 0, self.first, jnp.where(self.long, self.parked(1), self.kept(2)))


def nt(a, b):
    return lax.dot_general(a, b, (((1,), (1,)), ((), ())), preferred_element_type=jnp.float32)


def nn(a, b):
    return lax.dot_general(a, b, (((1,), (0,)), ((), ())), preferred_element_type=jnp.float32)


def tn(a, b):
    return lax.dot_general(a, b, (((0,), (0,)), ((), ())), preferred_element_type=jnp.float32)


def attention_grads(q, k, v, grads, valids, joins):
    count = len(q)
    key_ids = lax.broadcasted_iota(jnp.int32, (BLK, BLK), 0)
    query_ids = lax.broadcasted_iota(jnp.int32, (BLK, BLK), 1)
    low = lambda x: x.astype(jnp.bfloat16)
    grads = [jnp.where(key_ids < valids[j], grads[j], jnp.zeros((), jnp.bfloat16)) for j in range(count)]
    both = lambda x, j: jnp.concatenate(x[j : j + 2]) if j + 1 < count else x[j]
    left, right = (lambda x: x[:, :BLK]), (lambda x: x[:, BLK:])

    scores = [nt(k[j], both(q, j)) for j in range(count)]
    prob_grad = [nt(v[j], both(grads, j)) for j in range(count)]
    attend, score_grad = [], []
    for j in range(count):
        here = jnp.where((key_ids <= query_ids) & (key_ids < valids[j]), left(scores[j]) * FACTOR2, -jnp.inf)
        here_grad = left(prob_grad[j])
        top = jnp.max(here, axis=0, keepdims=True)
        if j:
            before = jnp.where(joins[j], right(scores[j - 1]) * FACTOR2, -jnp.inf)
            before_grad = right(prob_grad[j - 1])
            top = jnp.maximum(top, jnp.max(before, axis=0, keepdims=True))
        here = jnp.exp2(here - top)
        total = jnp.sum(here, axis=0, keepdims=True)
        if j:
            before = jnp.exp2(before - top)
            total = total + jnp.sum(before, axis=0, keepdims=True)
        scale = 1.0 / total
        here = here * scale
        row_dot = jnp.sum(here * here_grad, axis=0, keepdims=True)
        if j:
            before = before * scale
            row_dot = row_dot + jnp.sum(before * before_grad, axis=0, keepdims=True)
            attend[j - 1].append(low(before))
            score_grad[j - 1].append(low(before * (before_grad - row_dot)))
        attend.append([low(here)])
        score_grad.append([low(here * (here_grad - row_dot))])
    wide = lambda x: jnp.concatenate(x, axis=1) if len(x) > 1 else x[0]
    dv = [low(nn(wide(attend[j]), both(grads, j))) for j in range(count)]
    dk = [low(nn(wide(score_grad[j]), both(q, j)) * FACTOR) for j in range(count)]
    dq = []
    for j in range(count):
        if j:
            weights, keys = jnp.concatenate([score_grad[j - 1][1], score_grad[j][0]]), jnp.concatenate(k[j - 1 : j + 1])
        else:
            weights, keys = score_grad[0][0], k[0]
        dq.append(low(tn(weights, keys) * FACTOR))
    return dq, dk, dv


def worth(flops):
    return pl.CostEstimate(flops=flops, bytes_accessed=1 << 20, transcendentals=0)


def columns(head, part):
    return slice(head * HW + part * HD, head * HW + (part + 1) * HD)


def kept_kernel(lengths, evicted, rows, g0, g1, g2, early, third):
    plan = Plan(lengths, evicted)
    blocks = [plan.kept(j) for j in range(KB)]
    valids = [plan.valid(b) for b in blocks]
    segments = [plan.segment(b) for b in blocks]
    joins = [None] + [(segments[j] == segments[j - 1]) & jnp.logical_not(plan.long) for j in range(1, KB)]
    for head in range(KEPT_STEP):
        q, k, v = ([rows[j * BLK : (j + 1) * BLK, columns(head, p)] for j in range(KB)] for p in range(3))
        grads = [g[:, head * HD : (head + 1) * HD] for g in (g0, g1, g2)]
        for part, made in enumerate(attention_grads(q, k, v, grads, valids, joins)):
            early[0:BLK, columns(head, part)] = made[0]
            early[BLK : 2 * BLK, columns(head, part)] = made[1]
            third[:, columns(head, part)] = made[2]


def kept_part(lengths, evicted, kept_rows, grad_out, first, heads):
    at = first // KEPT_STEP
    grad_spec = lambda j: pl.BlockSpec(
        (BLK, KEPT_STEP * HD), lambda i, ln, ev: (Plan(ln, ev).kept(j), at + i)
    )
    return pl.pallas_call(
        kept_kernel,
        grid_spec=pltpu.PrefetchScalarGridSpec(
            num_scalar_prefetch=2,
            grid=(heads // KEPT_STEP,),
            in_specs=[pl.BlockSpec((KB * BLK, KEPT_STEP * HW), lambda i, ln, ev: (0, at + i))]
            + [grad_spec(j) for j in range(KB)],
            out_specs=[
                pl.BlockSpec((2 * BLK, KEPT_STEP * HW), lambda i, ln, ev: (0, i)),
                pl.BlockSpec((BLK, KEPT_STEP * HW), lambda i, ln, ev: (0, i)),
            ],
        ),
        out_shape=[
            jax.ShapeDtypeStruct((2 * BLK, heads * HW), jnp.bfloat16),
            jax.ShapeDtypeStruct((BLK, heads * HW), jnp.bfloat16),
        ],
        compiler_params=pltpu.CompilerParams(vmem_limit_bytes=VMEM),
        cost_estimate=worth(heads * KEPT_COST),
        name="kept_grads",
    )(lengths, evicted, kept_rows, grad_out, grad_out, grad_out)


def parked_kernel(lengths, evicted, quarters, r0, r1, r2, r3, g0, g1, third, late, rows):
    plan = Plan(lengths, evicted)
    quarter = BLK // 2
    for d, piece in enumerate((r0, r1, r2, r3)):
        start = pl.multiple_of(quarters[d] * quarter, quarter)
        rows[pl.ds(start, quarter), :] = piece[...]
    valids = [plan.valid(plan.parked(j)) for j in range(2)]
    joins = [None, plan.long]
    for head in range(PARKED_STEP):
        q, k, v = ([rows[j * BLK : (j + 1) * BLK, columns(head, p)] for j in range(2)] for p in range(3))
        grads = [g[:, head * HD : (head + 1) * HD] for g in (g0, g1)]
        grads[1] = jnp.where(plan.long, grads[1], jnp.zeros((), jnp.bfloat16))
        for part, made in enumerate(attention_grads(q, k, v, grads, valids, joins)):
            late[0:BLK, columns(head, part)] = made[0]
            late[BLK : 2 * BLK, columns(head, part)] = jnp.where(
                plan.long, made[1], third[:, columns(head, part)]
            )


def parked_part(lengths, evicted, quarters, pieces, grad_out, third, first, heads, flops):
    at = first // PARKED_STEP
    grad_spec = lambda j: pl.BlockSpec(
        (BLK, PARKED_STEP * HD), lambda i, ln, ev, sh: (Plan(ln, ev).parked(j), at + i)
    )
    return pl.pallas_call(
        parked_kernel,
        grid_spec=pltpu.PrefetchScalarGridSpec(
            num_scalar_prefetch=3,
            grid=(heads // PARKED_STEP,),
            in_specs=[pl.BlockSpec((BLK // 2, PARKED_STEP * HW), lambda i, ln, ev, sh: (0, i))] * 2
            + [pl.BlockSpec((BLK // 2, PARKED_STEP * HW), lambda i, ln, ev, sh: (0, at + i))] * 2
            + [grad_spec(j) for j in range(2)]
            + [pl.BlockSpec((BLK, PARKED_STEP * HW), lambda i, ln, ev, sh: (0, at + i))],
            out_specs=pl.BlockSpec((2 * BLK, PARKED_STEP * HW), lambda i, ln, ev, sh: (0, i)),
            scratch_shapes=[pltpu.VMEM((2 * BLK, PARKED_STEP * HW), jnp.bfloat16)],
        ),
        out_shape=jax.ShapeDtypeStruct((2 * BLK, heads * HW), jnp.bfloat16),
        compiler_params=pltpu.CompilerParams(vmem_limit_bytes=VMEM),
        cost_estimate=worth(heads * flops),
        name="parked_grads",
    )(lengths, evicted, quarters, *pieces, grad_out, grad_out, third)


def place_kernel(slots, firsts, flagged, lengths, evicted, flag, *refs):
    count = len(slots)
    pieces, (out, *rooms), (into, outof) = refs[:count], refs[-count - 3 : -2], refs[-2:]
    plan = Plan(lengths, evicted)

    def copies(n):
        pairs = []
        for slot in range(2):
            rows = pl.ds(slot * BLK, BLK)
            start = pl.multiple_of(slots[n](plan, slot) * BLK, BLK)
            there = out.at[pl.ds(start, BLK), pl.ds(firsts[n] * HW, pieces[n].shape[1])]
            pairs.append(
                (
                    pltpu.make_async_copy(pieces[n].at[rows, :], rooms[n].at[rows, :], into.at[n, slot]),
                    pltpu.make_async_copy(rooms[n].at[rows, :], there, outof.at[n, slot]),
                )
            )
        return pairs

    def move(n):
        pairs = copies(n)
        for fetch, _ in pairs:
            fetch.start()
        for fetch, store in pairs:
            fetch.wait()
            store.start()
        for _, store in pairs:
            store.wait()

    for n in range(count):
        if flagged[n]:
            pl.when(flag[0] > 0)(functools.partial(move, n))
        else:
            move(n)


def place(lengths, evicted, flag, out, total, *items):
    pieces, slots, firsts, flagged = zip(*items)
    base = (lengths, evicted, flag, *pieces) + (() if out is None else (out,))
    smem, hbm = pl.BlockSpec(memory_space=pltpu.SMEM), pl.BlockSpec(memory_space=pltpu.HBM)
    count = len(items)
    return pl.pallas_call(
        functools.partial(place_kernel, slots, firsts, flagged),
        in_specs=[smem] * 3 + [hbm] * (len(base) - 3),
        out_specs=hbm,
        scratch_shapes=[pltpu.VMEM(piece.shape, piece.dtype) for piece in pieces]
        + [pltpu.SemaphoreType.DMA((count, 2)), pltpu.SemaphoreType.DMA((count, 2))],
        out_shape=jax.ShapeDtypeStruct(total, jnp.bfloat16),
        input_output_aliases={} if out is None else {3 + count: 0},
        compiler_params=pltpu.CompilerParams(vmem_limit_bytes=VMEM),
        name="place_rows",
    )(*base)


def shards(kept_rows, parked_rows, grad_out, lengths, evicted):
    sections, peers = lax.axis_size("section"), lax.axis_size("tp")
    half = sections // 2
    ring = 2 * peers
    total = (grad_out.shape[0], kept_rows.shape[1])
    share = total[1]
    spot = 2 * lax.axis_index("tp") + lax.axis_index("section") // half

    def shifted(rows, hops):
        pairs = []
        for s in range(sections):
            for t in range(peers):
                to = (2 * t + s // half + hops) % ring
                pairs.append((s * peers + t, ((s + half) % sections) * peers + to // 2))
        return lax.ppermute(rows, ("section", "tp"), pairs)

    def passed_back(rows, within=sections):
        pairs = [(i, i // within * within + (i - 1) % within) for i in range(sections)]
        return lax.ppermute(rows, "section", pairs)

    def across_ends(rows):
        return lax.ppermute(rows, "section", [(half - 1, sections - 1), (sections - 1, half - 1)])

    next_evicted = passed_back(evicted)
    last = (lax.rem(lax.axis_index("section"), half) == half - 1).astype(jnp.int32).reshape(1)

    def parked_piece(hops, first, heads):
        to = lax.rem(spot + hops + ring, ring) // 2
        rows = lax.dynamic_slice(
            parked_rows, (0, to * share + first * HW), (parked_rows.shape[0], heads * HW)
        )
        return shifted(rows, hops)

    def once(value, *done):
        return lax.optimization_barrier((value, *done))[0]

    quarters = jnp.stack([lax.rem(spot - hops + ring, ring) // 2 for hops in HOPS]).astype(jnp.int32)
    p1, p2 = PARKED_CHUNKS
    far, near = HOPS[:2], HOPS[2:]
    z1 = [parked_piece(hops, 0, p1) for hops in far]
    both = [parked_piece(hops, 0, p1 + p2) for hops in near]
    z2 = [parked_piece(hops, p1, p2) for hops in far]
    early, third = kept_part(lengths, evicted, kept_rows, grad_out, 0, p1 + p2)
    x1 = passed_back(once(early, next_evicted), half)
    late1 = parked_part(lengths, evicted, quarters, z1 + both, grad_out, third, 0, p1, PARKED_COST)
    x2 = passed_back(once(late1, x1))
    late2 = parked_part(once(lengths, late1), evicted, quarters, z2 + both, grad_out, third, p1, p2, LATE_COST)
    x3 = passed_back(late2)
    x1_ends = across_ends(once(x1, late1))
    out = place(lengths, next_evicted, last, None, total, (x1, Plan.kept, 0, False))
    out = place(lengths, next_evicted, last, out, total, (x2, Plan.late, 0, False), (x1_ends, Plan.kept, 0, True))
    return place(lengths, next_evicted, last, out, total, (x3, Plan.late, p1, False))


def solution(mesh):
    in_specs = (
        P("section", "tp"),
        P(("section", "tp"), None),
        P("section", "tp"),
        P(),
        P("section"),
    )
    out_specs = P("section", "tp")
    return jax.shard_map(shards, mesh=mesh, in_specs=in_specs, out_specs=out_specs, check_vma=False)
```

```python
import functools

import jax
import jax.numpy as jnp
from jax import lax
from jax.experimental import pallas as pl
from jax.experimental.pallas import tpu as pltpu
from jax.sharding import PartitionSpec as P

HD = 128
BLK = 128
KB = 3
HW = 3 * HD
FACTOR = HD**-0.5
FACTOR2 = FACTOR * 1.4426950408889634
KEPT_STEP = 4
PARKED_STEP = 6
VMEM = 20 << 20
HOPS = (3, -3, 1, -1)
KEPT_COST = 1000_000_000
LATE_COSTS = (8000_000_000,)
PLACE_COST = 1000_000_000
PARKED_COST = 4000_000_000
PARKED_CHUNKS = (6, 6)
LAST_CHUNKS = (6,)


def pick(index, values):
    return jnp.where(index == 0, values[0], jnp.where(index == 1, values[1], values[2]))


class Plan:
    def __init__(self, lengths, evicted):
        self.lengths = [lengths[m] for m in range(3)]
        counts = [lax.shift_right_logical(n + (BLK - 1), 7) for n in self.lengths]
        self.starts = [jnp.int32(0), counts[0], counts[0] + counts[1]]
        which = evicted[0]
        self.first = pick(which, self.starts)
        self.span = pick(which, counts)
        self.long = self.span > 1

    def segment(self, block):
        return (block >= self.starts[1]).astype(jnp.int32) + (block >= self.starts[2]).astype(jnp.int32)

    def valid(self, block):
        m = self.segment(block)
        return jnp.clip(pick(m, self.lengths) - BLK * (block - pick(m, self.starts)), 0, BLK)

    def kept(self, slot):
        return jnp.minimum(slot + jnp.where(slot >= self.first, self.span, 0), 3)

    def parked(self, slot):
        return jnp.minimum(self.first + slot, 3)

    def late(self, slot):
        return jnp.where(slot == 0, self.first, jnp.where(self.long, self.parked(1), self.kept(2)))


def nt(a, b):
    return lax.dot_general(a, b, (((1,), (1,)), ((), ())), preferred_element_type=jnp.float32)


def nn(a, b):
    return lax.dot_general(a, b, (((1,), (0,)), ((), ())), preferred_element_type=jnp.float32)


def tn(a, b):
    return lax.dot_general(a, b, (((0,), (0,)), ((), ())), preferred_element_type=jnp.float32)


def attention_grads(q, k, v, grads, valids, joins):
    count = len(q)
    key_ids = lax.broadcasted_iota(jnp.int32, (BLK, BLK), 0)
    query_ids = lax.broadcasted_iota(jnp.int32, (BLK, BLK), 1)
    low = lambda x: x.astype(jnp.bfloat16)
    grads = [jnp.where(key_ids < valids[j], grads[j], jnp.zeros((), jnp.bfloat16)) for j in range(count)]
    both = lambda x, j: jnp.concatenate(x[j : j + 2]) if j + 1 < count else x[j]
    left, right = (lambda x: x[:, :BLK]), (lambda x: x[:, BLK:])

    scores = [nt(k[j], both(q, j)) for j in range(count)]
    prob_grad = [nt(v[j], both(grads, j)) for j in range(count)]
    attend, score_grad = [], []
    for j in range(count):
        here = jnp.where((key_ids <= query_ids) & (key_ids < valids[j]), left(scores[j]) * FACTOR2, -jnp.inf)
        here_grad = left(prob_grad[j])
        top = jnp.max(here, axis=0, keepdims=True)
        if j:
            before = jnp.where(joins[j], right(scores[j - 1]) * FACTOR2, -jnp.inf)
            before_grad = right(prob_grad[j - 1])
            top = jnp.maximum(top, jnp.max(before, axis=0, keepdims=True))
        here = jnp.exp2(here - top)
        total = jnp.sum(here, axis=0, keepdims=True)
        if j:
            before = jnp.exp2(before - top)
            total = total + jnp.sum(before, axis=0, keepdims=True)
        scale = 1.0 / total
        here = here * scale
        row_dot = jnp.sum(here * here_grad, axis=0, keepdims=True)
        if j:
            before = before * scale
            row_dot = row_dot + jnp.sum(before * before_grad, axis=0, keepdims=True)
            attend[j - 1].append(low(before))
            score_grad[j - 1].append(low(before * (before_grad - row_dot)))
        attend.append([low(here)])
        score_grad.append([low(here * (here_grad - row_dot))])
    wide = lambda x: jnp.concatenate(x, axis=1) if len(x) > 1 else x[0]
    dv = [low(nn(wide(attend[j]), both(grads, j))) for j in range(count)]
    dk = [low(nn(wide(score_grad[j]), both(q, j)) * FACTOR) for j in range(count)]
    dq = []
    for j in range(count):
        if j:
            weights, keys = jnp.concatenate([score_grad[j - 1][1], score_grad[j][0]]), jnp.concatenate(k[j - 1 : j + 1])
        else:
            weights, keys = score_grad[0][0], k[0]
        dq.append(low(tn(weights, keys) * FACTOR))
    return dq, dk, dv


def worth(flops):
    return pl.CostEstimate(flops=flops, bytes_accessed=1 << 20, transcendentals=0)


def in_hbm(x):
    return pltpu.with_memory_space_constraint(x, pltpu.HBM)


def columns(head, part):
    return slice(head * HW + part * HD, head * HW + (part + 1) * HD)


def kept_kernel(lengths, evicted, rows, g0, g1, g2, early, third):
    plan = Plan(lengths, evicted)
    blocks = [plan.kept(j) for j in range(KB)]
    valids = [plan.valid(b) for b in blocks]
    segments = [plan.segment(b) for b in blocks]
    joins = [None] + [(segments[j] == segments[j - 1]) & jnp.logical_not(plan.long) for j in range(1, KB)]
    for head in range(KEPT_STEP):
        q, k, v = ([rows[j * BLK : (j + 1) * BLK, columns(head, p)] for j in range(KB)] for p in range(3))
        grads = [g[:, head * HD : (head + 1) * HD] for g in (g0, g1, g2)]
        for part, made in enumerate(attention_grads(q, k, v, grads, valids, joins)):
            early[0:BLK, columns(head, part)] = made[0]
            early[BLK : 2 * BLK, columns(head, part)] = made[1]
            third[:, columns(head, part)] = made[2]


def kept_part(lengths, evicted, kept_rows, grad_out, first, heads):
    at = first // KEPT_STEP
    grad_spec = lambda j: pl.BlockSpec(
        (BLK, KEPT_STEP * HD), lambda i, ln, ev: (Plan(ln, ev).kept(j), at + i)
    )
    return pl.pallas_call(
        kept_kernel,
        grid_spec=pltpu.PrefetchScalarGridSpec(
            num_scalar_prefetch=2,
            grid=(heads // KEPT_STEP,),
            in_specs=[pl.BlockSpec((KB * BLK, KEPT_STEP * HW), lambda i, ln, ev: (0, at + i))]
            + [grad_spec(j) for j in range(KB)],
            out_specs=[
                pl.BlockSpec((2 * BLK, KEPT_STEP * HW), lambda i, ln, ev: (0, i)),
                pl.BlockSpec((BLK, KEPT_STEP * HW), lambda i, ln, ev: (0, i)),
            ],
        ),
        out_shape=[
            jax.ShapeDtypeStruct((2 * BLK, heads * HW), jnp.bfloat16),
            jax.ShapeDtypeStruct((BLK, heads * HW), jnp.bfloat16),
        ],
        compiler_params=pltpu.CompilerParams(vmem_limit_bytes=VMEM),
        cost_estimate=worth(heads * KEPT_COST),
        name="kept_grads",
    )(lengths, evicted, in_hbm(kept_rows), *[in_hbm(grad_out)] * 3)


def parked_kernel(ats, lengths, evicted, quarters, r0, r1, r2, r3, g0, g1, third, late, rows):
    plan = Plan(lengths, evicted)
    quarter = BLK // 2
    for d, piece in enumerate((r0, r1, r2, r3)):
        start = pl.multiple_of(quarters[d] * quarter, quarter)
        width = rows.shape[1]
        first = pl.multiple_of((ats[d] + pl.program_id(0)) * width, BLK)
        rows[pl.ds(start, quarter), :] = piece[:, pl.ds(first, width)]
    valids = [plan.valid(plan.parked(j)) for j in range(2)]
    joins = [None, plan.long]
    for head in range(rows.shape[1] // HW):
        q, k, v = ([rows[j * BLK : (j + 1) * BLK, columns(head, p)] for j in range(2)] for p in range(3))
        grads = [g[:, head * HD : (head + 1) * HD] for g in (g0, g1)]
        grads[1] = jnp.where(plan.long, grads[1], jnp.zeros((), jnp.bfloat16))
        for part, made in enumerate(attention_grads(q, k, v, grads, valids, joins)):
            late[0:BLK, columns(head, part)] = made[0]
            late[BLK : 2 * BLK, columns(head, part)] = jnp.where(
                plan.long, made[1], third[:, columns(head, part)]
            )


def parked_part(lengths, evicted, quarters, pieces, grad_out, third, first, heads, flops, far_first=0):
    step = min(PARKED_STEP, heads)
    at, far_at = first // step, (first - far_first) // step
    grad_spec = lambda j: pl.BlockSpec(
        (BLK, step * HD), lambda i, ln, ev, sh: (Plan(ln, ev).parked(j), at + i)
    )
    return pl.pallas_call(
        functools.partial(parked_kernel, (far_at, far_at, at, at)),
        grid_spec=pltpu.PrefetchScalarGridSpec(
            num_scalar_prefetch=3,
            grid=(heads // step,),
            in_specs=[pl.BlockSpec(memory_space=pltpu.VMEM)] * 4
            + [grad_spec(j) for j in range(2)]
            + [pl.BlockSpec((BLK, step * HW), lambda i, ln, ev, sh: (0, at + i))],
            out_specs=pl.BlockSpec((2 * BLK, step * HW), lambda i, ln, ev, sh: (0, i)),
            scratch_shapes=[pltpu.VMEM((2 * BLK, step * HW), jnp.bfloat16)],
        ),
        out_shape=jax.ShapeDtypeStruct((2 * BLK, heads * HW), jnp.bfloat16),
        compiler_params=pltpu.CompilerParams(vmem_limit_bytes=VMEM),
        cost_estimate=worth(heads * flops),
        name="parked_grads",
    )(lengths, evicted, quarters, *pieces, *[in_hbm(grad_out)] * 2, in_hbm(third))


def place_kernel(slots, firsts, flagged, lengths, evicted, flag, *refs):
    count = len(slots)
    pieces, (out, sems) = refs[:count], refs[-2:]
    plan = Plan(lengths, evicted)

    def store(n, slot):
        start = pl.multiple_of(slots[n](plan, slot) * BLK, BLK)
        return pltpu.make_async_copy(
            pieces[n].at[pl.ds(slot * BLK, BLK), :],
            out.at[pl.ds(start, BLK), pl.ds(firsts[n] * HW, pieces[n].shape[1])],
            sems.at[n, slot],
        )

    def begin(n):
        for slot in range(2):
            store(n, slot).start()

    def finish(n):
        for slot in range(2):
            store(n, slot).wait()

    for step in (begin, finish):
        for n in range(count):
            run = functools.partial(step, n)
            if flagged[n]:
                pl.when(flag[0] > 0)(run)
            else:
                run()


def place(lengths, evicted, flag, out, total, *items):
    pieces, slots, firsts, flagged = zip(*items)
    base = (lengths, evicted, flag, *pieces) + (() if out is None else (out,))
    smem, free = pl.BlockSpec(memory_space=pltpu.SMEM), pl.BlockSpec(memory_space=pl.ANY)
    count = len(items)
    return pl.pallas_call(
        functools.partial(place_kernel, slots, firsts, flagged),
        in_specs=[smem] * 3 + [free] * (len(base) - 3),
        out_specs=free,
        scratch_shapes=[pltpu.SemaphoreType.DMA((count, 2))],
        out_shape=jax.ShapeDtypeStruct(total, jnp.bfloat16),
        input_output_aliases={} if out is None else {3 + count: 0},
        compiler_params=pltpu.CompilerParams(vmem_limit_bytes=1 << 20),
        cost_estimate=worth(PLACE_COST),
        name="place_rows",
    )(*base)


def shards(kept_rows, parked_rows, grad_out, lengths, evicted):
    sections, peers = lax.axis_size("section"), lax.axis_size("tp")
    half = sections // 2
    ring = 2 * peers
    total = (grad_out.shape[0], kept_rows.shape[1])
    share = total[1]
    spot = 2 * lax.axis_index("tp") + lax.axis_index("section") // half

    def shifted(rows, hops):
        pairs = []
        for s in range(sections):
            for t in range(peers):
                to = (2 * t + s // half + hops) % ring
                pairs.append((s * peers + t, ((s + half) % sections) * peers + to // 2))
        return lax.ppermute(rows, ("section", "tp"), pairs)

    def passed_back(rows, within=sections):
        pairs = [(i, i // within * within + (i - 1) % within) for i in range(sections)]
        return lax.ppermute(rows, "section", pairs)

    def across_ends(rows):
        return lax.ppermute(rows, "section", [(half - 1, sections - 1), (sections - 1, half - 1)])

    next_evicted = passed_back(evicted)
    last = (lax.rem(lax.axis_index("section"), half) == half - 1).astype(jnp.int32).reshape(1)

    def parked_piece(hops, first, heads):
        to = lax.rem(spot + hops + ring, ring) // 2
        rows = lax.dynamic_slice(
            parked_rows, (0, to * share + first * HW), (parked_rows.shape[0], heads * HW)
        )
        return shifted(rows, hops)

    def once(value, *done):
        return lax.optimization_barrier((value, *done))[0]

    quarters = jnp.stack([lax.rem(spot - hops + ring, ring) // 2 for hops in HOPS]).astype(jnp.int32)
    p1, p2 = PARKED_CHUNKS
    far, near = HOPS[:2], HOPS[2:]
    z1 = [parked_piece(hops, 0, p1) for hops in far]
    both = [parked_piece(hops, 0, p1 + p2) for hops in near]
    z2 = [parked_piece(hops, p1, p2) for hops in far]
    early, third = kept_part(lengths, evicted, kept_rows, grad_out, 0, p1 + p2)
    x1 = passed_back(once(early, next_evicted), half)
    late1 = parked_part(lengths, evicted, quarters, z1 + both, grad_out, third, 0, p1, PARKED_COST)
    x2 = passed_back(once(late1, x1))
    x1_ends = across_ends(once(x1, late1))
    out = place(lengths, next_evicted, last, None, total, (x1, Plan.kept, 0, False))
    pieces = []
    before, first = (late1, out), p1
    for heads, flops in zip(LAST_CHUNKS, LATE_COSTS):
        late = parked_part(
            once(lengths, *before), evicted, quarters, z2 + both, grad_out, third, first, heads, flops, p1
        )
        pieces.append((passed_back(late), Plan.late, first, False))
        before, first = (late, x2), first + heads
    out = place(lengths, next_evicted, last, out, total, (x2, Plan.late, 0, False))
    return place(lengths, next_evicted, last, out, total, (x1_ends, Plan.kept, 0, True), *pieces)


def solution(mesh):
    in_specs = (
        P("section", "tp"),
        P(("section", "tp"), None),
        P("section", "tp"),
        P(),
        P("section"),
    )
    out_specs = P("section", "tp")
    return jax.shard_map(shards, mesh=mesh, in_specs=in_specs, out_specs=out_specs, check_vma=False)
```

```python
import functools

import jax
import jax.numpy as jnp
from jax import lax
from jax.experimental import pallas as pl
from jax.experimental.pallas import tpu as pltpu
from jax.sharding import PartitionSpec as P

HD = 128
BLK = 128
KB = 3
HW = 3 * HD
FACTOR = HD**-0.5
FACTOR2 = FACTOR * 1.4426950408889634
KEPT_STEP = 4
PARKED_STEP = 6
VMEM = 20 << 20
HOPS = (3, -3, 1, -1)
KEPT_COST = 1000_000_000
LATE_COST = 8000_000_000
PLACE_COST = 1000_000_000
PARKED_COST = 4000_000_000
PARKED_CHUNKS = (6, 6)


def pick(index, values):
    return jnp.where(index == 0, values[0], jnp.where(index == 1, values[1], values[2]))


class Plan:
    def __init__(self, lengths, evicted):
        self.lengths = [lengths[m] for m in range(3)]
        counts = [lax.shift_right_logical(n + (BLK - 1), 7) for n in self.lengths]
        self.starts = [jnp.int32(0), counts[0], counts[0] + counts[1]]
        which = evicted[0]
        self.first = pick(which, self.starts)
        self.span = pick(which, counts)
        self.long = self.span > 1

    def segment(self, block):
        return (block >= self.starts[1]).astype(jnp.int32) + (block >= self.starts[2]).astype(jnp.int32)

    def valid(self, block):
        m = self.segment(block)
        return jnp.clip(pick(m, self.lengths) - BLK * (block - pick(m, self.starts)), 0, BLK)

    def kept(self, slot):
        return jnp.minimum(slot + jnp.where(slot >= self.first, self.span, 0), 3)

    def parked(self, slot):
        return jnp.minimum(self.first + slot, 3)

    def late(self, slot):
        return jnp.where(slot == 0, self.first, jnp.where(self.long, self.parked(1), self.kept(2)))


def nt(a, b):
    return lax.dot_general(a, b, (((1,), (1,)), ((), ())), preferred_element_type=jnp.float32)


def nn(a, b):
    return lax.dot_general(a, b, (((1,), (0,)), ((), ())), preferred_element_type=jnp.float32)


def tn(a, b):
    return lax.dot_general(a, b, (((0,), (0,)), ((), ())), preferred_element_type=jnp.float32)


def attention_grads(q, k, v, grads, valids, joins):
    count = len(q)
    key_ids = lax.broadcasted_iota(jnp.int32, (BLK, BLK), 0)
    query_ids = lax.broadcasted_iota(jnp.int32, (BLK, BLK), 1)
    low = lambda x: x.astype(jnp.bfloat16)
    grads = [jnp.where(key_ids < valids[j], grads[j], jnp.zeros((), jnp.bfloat16)) for j in range(count)]
    both = lambda x, j: jnp.concatenate(x[j : j + 2]) if j + 1 < count else x[j]
    left, right = (lambda x: x[:, :BLK]), (lambda x: x[:, BLK:])

    scores = [nt(k[j], both(q, j)) for j in range(count)]
    prob_grad = [nt(v[j], both(grads, j)) for j in range(count)]
    attend, score_grad = [], []
    for j in range(count):
        here = jnp.where((key_ids <= query_ids) & (key_ids < valids[j]), left(scores[j]) * FACTOR2, -jnp.inf)
        here_grad = left(prob_grad[j])
        top = jnp.max(here, axis=0, keepdims=True)
        if j:
            before = jnp.where(joins[j], right(scores[j - 1]) * FACTOR2, -jnp.inf)
            before_grad = right(prob_grad[j - 1])
            top = jnp.maximum(top, jnp.max(before, axis=0, keepdims=True))
        here = jnp.exp2(here - top)
        total = jnp.sum(here, axis=0, keepdims=True)
        if j:
            before = jnp.exp2(before - top)
            total = total + jnp.sum(before, axis=0, keepdims=True)
        scale = 1.0 / total
        here = here * scale
        row_dot = jnp.sum(here * here_grad, axis=0, keepdims=True)
        if j:
            before = before * scale
            row_dot = row_dot + jnp.sum(before * before_grad, axis=0, keepdims=True)
            attend[j - 1].append(low(before))
            score_grad[j - 1].append(low(before * (before_grad - row_dot)))
        attend.append([low(here)])
        score_grad.append([low(here * (here_grad - row_dot))])
    wide = lambda x: jnp.concatenate(x, axis=1) if len(x) > 1 else x[0]
    dv = [low(nn(wide(attend[j]), both(grads, j))) for j in range(count)]
    dk = [low(nn(wide(score_grad[j]), both(q, j)) * FACTOR) for j in range(count)]
    dq = []
    for j in range(count):
        if j:
            weights, keys = jnp.concatenate([score_grad[j - 1][1], score_grad[j][0]]), jnp.concatenate(k[j - 1 : j + 1])
        else:
            weights, keys = score_grad[0][0], k[0]
        dq.append(low(tn(weights, keys) * FACTOR))
    return dq, dk, dv


def worth(flops):
    return pl.CostEstimate(flops=flops, bytes_accessed=1 << 20, transcendentals=0)


def in_hbm(x):
    return pltpu.with_memory_space_constraint(x, pltpu.HBM)


def columns(head, part):
    return slice(head * HW + part * HD, head * HW + (part + 1) * HD)


def kept_kernel(lengths, evicted, rows, g0, g1, g2, early, third):
    plan = Plan(lengths, evicted)
    blocks = [plan.kept(j) for j in range(KB)]
    valids = [plan.valid(b) for b in blocks]
    segments = [plan.segment(b) for b in blocks]
    joins = [None] + [(segments[j] == segments[j - 1]) & jnp.logical_not(plan.long) for j in range(1, KB)]
    for head in range(KEPT_STEP):
        q, k, v = ([rows[j * BLK : (j + 1) * BLK, columns(head, p)] for j in range(KB)] for p in range(3))
        grads = [g[:, head * HD : (head + 1) * HD] for g in (g0, g1, g2)]
        for part, made in enumerate(attention_grads(q, k, v, grads, valids, joins)):
            early[0:BLK, columns(head, part)] = made[0]
            early[BLK : 2 * BLK, columns(head, part)] = made[1]
            third[:, columns(head, part)] = made[2]


def kept_part(lengths, evicted, kept_rows, grad_out, first, heads):
    at = first // KEPT_STEP
    grad_spec = lambda j: pl.BlockSpec(
        (BLK, KEPT_STEP * HD), lambda i, ln, ev: (Plan(ln, ev).kept(j), at + i)
    )
    return pl.pallas_call(
        kept_kernel,
        grid_spec=pltpu.PrefetchScalarGridSpec(
            num_scalar_prefetch=2,
            grid=(heads // KEPT_STEP,),
            in_specs=[pl.BlockSpec((KB * BLK, KEPT_STEP * HW), lambda i, ln, ev: (0, at + i))]
            + [grad_spec(j) for j in range(KB)],
            out_specs=[
                pl.BlockSpec((2 * BLK, KEPT_STEP * HW), lambda i, ln, ev: (0, i)),
                pl.BlockSpec((BLK, KEPT_STEP * HW), lambda i, ln, ev: (0, i)),
            ],
        ),
        out_shape=[
            jax.ShapeDtypeStruct((2 * BLK, heads * HW), jnp.bfloat16),
            pltpu.HBM((BLK, heads * HW), jnp.bfloat16),
        ],
        compiler_params=pltpu.CompilerParams(vmem_limit_bytes=VMEM),
        cost_estimate=worth(heads * KEPT_COST),
        name="kept_grads",
    )(lengths, evicted, in_hbm(kept_rows), *[in_hbm(grad_out)] * 3)


def parked_kernel(ats, lengths, evicted, quarters, r0, r1, r2, r3, g0, g1, third, late0, late1, rows):
    plan = Plan(lengths, evicted)
    quarter = BLK // 2
    for d, piece in enumerate((r0, r1, r2, r3)):
        start = pl.multiple_of(quarters[d] * quarter, quarter)
        width = rows.shape[1]
        first = pl.multiple_of((ats[d] + pl.program_id(0)) * width, BLK)
        rows[pl.ds(start, quarter), :] = piece[:, pl.ds(first, width)]
    valids = [plan.valid(plan.parked(j)) for j in range(2)]
    joins = [None, plan.long]
    for head in range(rows.shape[1] // HW):
        q, k, v = ([rows[j * BLK : (j + 1) * BLK, columns(head, p)] for j in range(2)] for p in range(3))
        grads = [g[:, head * HD : (head + 1) * HD] for g in (g0, g1)]
        grads[1] = jnp.where(plan.long, grads[1], jnp.zeros((), jnp.bfloat16))
        for part, made in enumerate(attention_grads(q, k, v, grads, valids, joins)):
            late0[:, columns(head, part)] = made[0]
            late1[:, columns(head, part)] = jnp.where(
                plan.long, made[1], third[:, columns(head, part)]
            )


def parked_part(lengths, evicted, quarters, pieces, grad_out, third, first, heads, flops, far_first=0):
    step = min(PARKED_STEP, heads)
    at, far_at = first // step, (first - far_first) // step
    grad_spec = lambda j: pl.BlockSpec(
        (BLK, step * HD), lambda i, ln, ev, sh: (Plan(ln, ev).parked(j), at + i)
    )
    return pl.pallas_call(
        functools.partial(parked_kernel, (far_at, far_at, at, at)),
        grid_spec=pltpu.PrefetchScalarGridSpec(
            num_scalar_prefetch=3,
            grid=(heads // step,),
            in_specs=[pl.BlockSpec(memory_space=pltpu.VMEM)] * 4
            + [grad_spec(j) for j in range(2)]
            + [pl.BlockSpec((BLK, step * HW), lambda i, ln, ev, sh: (0, at + i))],
            out_specs=[pl.BlockSpec((BLK, step * HW), lambda i, ln, ev, sh: (0, i))] * 2,
            scratch_shapes=[pltpu.VMEM((2 * BLK, step * HW), jnp.bfloat16)],
        ),
        out_shape=[jax.ShapeDtypeStruct((BLK, heads * HW), jnp.bfloat16)] * 2,
        compiler_params=pltpu.CompilerParams(vmem_limit_bytes=VMEM),
        cost_estimate=worth(heads * flops),
        name="parked_grads",
    )(lengths, evicted, quarters, *pieces, *[in_hbm(grad_out)] * 2, in_hbm(third))


def place_kernel(slots, firsts, flagged, lengths, evicted, flag, *refs):
    count = len(slots)
    pieces, (out, sems) = refs[:count], refs[-2:]
    plan = Plan(lengths, evicted)

    def store(n, slot):
        start = pl.multiple_of(slots[n](plan, slot) * BLK, BLK)
        return pltpu.make_async_copy(
            pieces[n].at[pl.ds(slot * BLK, BLK), :],
            out.at[pl.ds(start, BLK), pl.ds(firsts[n] * HW, pieces[n].shape[1])],
            sems.at[n, slot],
        )

    def begin(n):
        for slot in range(pieces[n].shape[0] // BLK):
            store(n, slot).start()

    def finish(n):
        for slot in range(pieces[n].shape[0] // BLK):
            store(n, slot).wait()

    for step in (begin, finish):
        for n in range(count):
            run = functools.partial(step, n)
            if flagged[n]:
                pl.when(flag[0] > 0)(run)
            else:
                run()


def place(lengths, evicted, flag, out, total, *items):
    pieces, slots, firsts, flagged = zip(*items)
    base = (lengths, evicted, flag, *pieces) + (() if out is None else (out,))
    smem, free = pl.BlockSpec(memory_space=pltpu.SMEM), pl.BlockSpec(memory_space=pl.ANY)
    count = len(items)
    return pl.pallas_call(
        functools.partial(place_kernel, slots, firsts, flagged),
        in_specs=[smem] * 3 + [free] * (len(base) - 3),
        out_specs=free,
        scratch_shapes=[pltpu.SemaphoreType.DMA((count, 2))],
        out_shape=jax.ShapeDtypeStruct(total, jnp.bfloat16),
        input_output_aliases={} if out is None else {3 + count: 0},
        compiler_params=pltpu.CompilerParams(vmem_limit_bytes=1 << 20),
        cost_estimate=worth(PLACE_COST),
        name="place_rows",
    )(*base)


def shards(kept_rows, parked_rows, grad_out, lengths, evicted):
    sections, peers = lax.axis_size("section"), lax.axis_size("tp")
    half = sections // 2
    ring = 2 * peers
    total = (grad_out.shape[0], kept_rows.shape[1])
    share = total[1]
    spot = 2 * lax.axis_index("tp") + lax.axis_index("section") // half

    def shifted(rows, hops):
        pairs = []
        for s in range(sections):
            for t in range(peers):
                to = (2 * t + s // half + hops) % ring
                pairs.append((s * peers + t, ((s + half) % sections) * peers + to // 2))
        return lax.ppermute(rows, ("section", "tp"), pairs)

    def passed_back(rows, within=sections):
        pairs = [(i, i // within * within + (i - 1) % within) for i in range(sections)]
        return lax.ppermute(rows, "section", pairs)

    def across_ends(rows):
        return lax.ppermute(rows, "section", [(half - 1, sections - 1), (sections - 1, half - 1)])

    next_evicted = passed_back(evicted)
    last = (lax.rem(lax.axis_index("section"), half) == half - 1).astype(jnp.int32).reshape(1)

    def parked_piece(hops, first, heads):
        to = lax.rem(spot + hops + ring, ring) // 2
        rows = lax.dynamic_slice(
            parked_rows, (0, to * share + first * HW), (parked_rows.shape[0], heads * HW)
        )
        return shifted(rows, hops)

    def once(value, *done):
        return lax.optimization_barrier((value, *done))[0]

    quarters = jnp.stack([lax.rem(spot - hops + ring, ring) // 2 for hops in HOPS]).astype(jnp.int32)
    p1, p2 = PARKED_CHUNKS
    far, near = HOPS[:2], HOPS[2:]
    z1 = [parked_piece(hops, 0, p1) for hops in far]
    both = [parked_piece(hops, 0, p1 + p2) for hops in near]
    z2 = [parked_piece(hops, p1, p2) for hops in far]
    early, third = kept_part(lengths, evicted, kept_rows, grad_out, 0, p1 + p2)
    x1 = passed_back(once(early, next_evicted), half)
    late1 = parked_part(lengths, evicted, quarters, z1 + both, grad_out, third, 0, p1, PARKED_COST)
    x2 = [passed_back(rows) for rows in late1]
    x1_ends = across_ends(once(x1, *late1))
    out = place(lengths, next_evicted, last, None, total, (x1, Plan.kept, 0, False))
    late2 = parked_part(
        once(lengths, *late1, out), evicted, quarters, z2 + both, grad_out, third, p1, p2, LATE_COST, p1
    )
    x3 = [passed_back(rows) for rows in late2]
    slots = (lambda plan, slot: plan.late(0), lambda plan, slot: plan.late(1))
    pieces = lambda rows, first: [(part, to, first, False) for part, to in zip(rows, slots)]
    out = place(lengths, next_evicted, last, out, total, *pieces(x2, 0))
    return place(lengths, next_evicted, last, out, total, (x1_ends, Plan.kept, 0, True), *pieces(x3, p1))


def solution(mesh):
    in_specs = (
        P("section", "tp"),
        P(("section", "tp"), None),
        P("section", "tp"),
        P(),
        P("section"),
    )
    out_specs = P("section", "tp")
    return jax.shard_map(shards, mesh=mesh, in_specs=in_specs, out_specs=out_specs, check_vma=False)
```

```python
import functools

import jax
import jax.numpy as jnp
from jax import lax
from jax.experimental import pallas as pl
from jax.experimental.pallas import tpu as pltpu
from jax.sharding import PartitionSpec as P

HD = 128
BLK = 128
KB = 3
HW = 3 * HD
FACTOR = HD**-0.5
FACTOR2 = FACTOR * 1.4426950408889634
KEPT_STEP = 4
PARKED_STEP = 6
VMEM = 20 << 20
HOPS = (3, -3, 1, -1)
KEPT_COST = 1000_000_000
LATE_COST = 8000_000_000
PLACE_COST = 1000_000_000
PARKED_COST = 4000_000_000
PARKED_CHUNKS = (6, 6)


def pick(index, values):
    return jnp.where(index == 0, values[0], jnp.where(index == 1, values[1], values[2]))


class Plan:
    def __init__(self, lengths, evicted):
        self.lengths = [lengths[m] for m in range(3)]
        counts = [lax.shift_right_logical(n + (BLK - 1), 7) for n in self.lengths]
        self.starts = [jnp.int32(0), counts[0], counts[0] + counts[1]]
        which = evicted[0]
        self.first = pick(which, self.starts)
        self.span = pick(which, counts)
        self.long = self.span > 1

    def segment(self, block):
        return (block >= self.starts[1]).astype(jnp.int32) + (block >= self.starts[2]).astype(jnp.int32)

    def valid(self, block):
        m = self.segment(block)
        return jnp.clip(pick(m, self.lengths) - BLK * (block - pick(m, self.starts)), 0, BLK)

    def kept(self, slot):
        return jnp.minimum(slot + jnp.where(slot >= self.first, self.span, 0), 3)

    def parked(self, slot):
        return jnp.minimum(self.first + slot, 3)

    def late(self, slot):
        return jnp.where(slot == 0, self.first, jnp.where(self.long, self.parked(1), self.kept(2)))


def nt(a, b):
    return lax.dot_general(a, b, (((1,), (1,)), ((), ())), preferred_element_type=jnp.float32)


def nn(a, b):
    return lax.dot_general(a, b, (((1,), (0,)), ((), ())), preferred_element_type=jnp.float32)


def tn(a, b):
    return lax.dot_general(a, b, (((0,), (0,)), ((), ())), preferred_element_type=jnp.float32)


def attention_grads(q, k, v, grads, valids, joins):
    count = len(q)
    key_ids = lax.broadcasted_iota(jnp.int32, (BLK, BLK), 0)
    query_ids = lax.broadcasted_iota(jnp.int32, (BLK, BLK), 1)
    low = lambda x: x.astype(jnp.bfloat16)
    grads = [jnp.where(key_ids < valids[j], grads[j], jnp.zeros((), jnp.bfloat16)) for j in range(count)]
    both = lambda x, j: jnp.concatenate(x[j : j + 2]) if j + 1 < count else x[j]
    left, right = (lambda x: x[:, :BLK]), (lambda x: x[:, BLK:])

    scores = [nt(k[j], both(q, j)) for j in range(count)]
    prob_grad = [nt(v[j], both(grads, j)) for j in range(count)]
    attend, score_grad = [], []
    for j in range(count):
        here = jnp.where((key_ids <= query_ids) & (key_ids < valids[j]), left(scores[j]) * FACTOR2, -jnp.inf)
        here_grad = left(prob_grad[j])
        top = jnp.max(here, axis=0, keepdims=True)
        if j:
            before = jnp.where(joins[j], right(scores[j - 1]) * FACTOR2, -jnp.inf)
            before_grad = right(prob_grad[j - 1])
            top = jnp.maximum(top, jnp.max(before, axis=0, keepdims=True))
        here = jnp.exp2(here - top)
        total = jnp.sum(here, axis=0, keepdims=True)
        if j:
            before = jnp.exp2(before - top)
            total = total + jnp.sum(before, axis=0, keepdims=True)
        scale = 1.0 / total
        here = here * scale
        row_dot = jnp.sum(here * here_grad, axis=0, keepdims=True)
        if j:
            before = before * scale
            row_dot = row_dot + jnp.sum(before * before_grad, axis=0, keepdims=True)
            attend[j - 1].append(low(before))
            score_grad[j - 1].append(low(before * (before_grad - row_dot)))
        attend.append([low(here)])
        score_grad.append([low(here * (here_grad - row_dot))])
    wide = lambda x: jnp.concatenate(x, axis=1) if len(x) > 1 else x[0]
    dv = [low(nn(wide(attend[j]), both(grads, j))) for j in range(count)]
    dk = [low(nn(wide(score_grad[j]), both(q, j)) * FACTOR) for j in range(count)]
    dq = []
    for j in range(count):
        if j:
            weights, keys = jnp.concatenate([score_grad[j - 1][1], score_grad[j][0]]), jnp.concatenate(k[j - 1 : j + 1])
        else:
            weights, keys = score_grad[0][0], k[0]
        dq.append(low(tn(weights, keys) * FACTOR))
    return dq, dk, dv


def worth(flops):
    return pl.CostEstimate(flops=flops, bytes_accessed=1 << 20, transcendentals=0)


def in_hbm(x):
    return pltpu.with_memory_space_constraint(x, pltpu.HBM)


def columns(head, part):
    return slice(head * HW + part * HD, head * HW + (part + 1) * HD)


def kept_kernel(lengths, evicted, rows, g0, g1, g2, early, third):
    plan = Plan(lengths, evicted)
    blocks = [plan.kept(j) for j in range(KB)]
    valids = [plan.valid(b) for b in blocks]
    segments = [plan.segment(b) for b in blocks]
    joins = [None] + [(segments[j] == segments[j - 1]) & jnp.logical_not(plan.long) for j in range(1, KB)]
    for head in range(KEPT_STEP):
        q, k, v = ([rows[j * BLK : (j + 1) * BLK, columns(head, p)] for j in range(KB)] for p in range(3))
        grads = [g[:, head * HD : (head + 1) * HD] for g in (g0, g1, g2)]
        for part, made in enumerate(attention_grads(q, k, v, grads, valids, joins)):
            early[0:BLK, columns(head, part)] = made[0]
            early[BLK : 2 * BLK, columns(head, part)] = made[1]
            third[:, columns(head, part)] = made[2]


def kept_part(lengths, evicted, kept_rows, grad_out, first, heads):
    at = first // KEPT_STEP
    grad_spec = lambda j: pl.BlockSpec(
        (BLK, KEPT_STEP * HD), lambda i, ln, ev: (Plan(ln, ev).kept(j), at + i)
    )
    return pl.pallas_call(
        kept_kernel,
        grid_spec=pltpu.PrefetchScalarGridSpec(
            num_scalar_prefetch=2,
            grid=(heads // KEPT_STEP,),
            in_specs=[pl.BlockSpec((KB * BLK, KEPT_STEP * HW), lambda i, ln, ev: (0, at + i))]
            + [grad_spec(j) for j in range(KB)],
            out_specs=[
                pl.BlockSpec((2 * BLK, KEPT_STEP * HW), lambda i, ln, ev: (0, i)),
                pl.BlockSpec((BLK, KEPT_STEP * HW), lambda i, ln, ev: (0, i)),
            ],
        ),
        out_shape=[
            jax.ShapeDtypeStruct((2 * BLK, heads * HW), jnp.bfloat16),
            pltpu.HBM((BLK, heads * HW), jnp.bfloat16),
        ],
        compiler_params=pltpu.CompilerParams(vmem_limit_bytes=VMEM),
        cost_estimate=worth(heads * KEPT_COST),
        name="kept_grads",
    )(lengths, evicted, in_hbm(kept_rows), *[in_hbm(grad_out)] * 3)


def parked_kernel(ats, lengths, evicted, quarters, r0, r1, r2, r3, g0, g1, third, late0, late1, rows):
    plan = Plan(lengths, evicted)
    quarter = BLK // 2
    for d, piece in enumerate((r0, r1, r2, r3)):
        start = pl.multiple_of(quarters[d] * quarter, quarter)
        width = rows.shape[1]
        first = pl.multiple_of((ats[d] + pl.program_id(0)) * width, BLK)
        rows[pl.ds(start, quarter), :] = piece[:, pl.ds(first, width)]
    valids = [plan.valid(plan.parked(j)) for j in range(2)]
    joins = [None, plan.long]
    for head in range(rows.shape[1] // HW):
        q, k, v = ([rows[j * BLK : (j + 1) * BLK, columns(head, p)] for j in range(2)] for p in range(3))
        grads = [g[:, head * HD : (head + 1) * HD] for g in (g0, g1)]
        grads[1] = jnp.where(plan.long, grads[1], jnp.zeros((), jnp.bfloat16))
        for part, made in enumerate(attention_grads(q, k, v, grads, valids, joins)):
            late0[:, columns(head, part)] = made[0]
            late1[:, columns(head, part)] = jnp.where(
                plan.long, made[1], third[:, columns(head, part)]
            )


def parked_part(lengths, evicted, quarters, pieces, grad_out, third, first, heads, flops, far_first=0):
    step = min(PARKED_STEP, heads)
    at, far_at = first // step, (first - far_first) // step
    grad_spec = lambda j: pl.BlockSpec(
        (BLK, step * HD), lambda i, ln, ev, sh: (Plan(ln, ev).parked(j), at + i)
    )
    return pl.pallas_call(
        functools.partial(parked_kernel, (far_at, far_at, at, at)),
        grid_spec=pltpu.PrefetchScalarGridSpec(
            num_scalar_prefetch=3,
            grid=(heads // step,),
            in_specs=[pl.BlockSpec(memory_space=pltpu.VMEM)] * 4
            + [grad_spec(j) for j in range(2)]
            + [pl.BlockSpec((BLK, step * HW), lambda i, ln, ev, sh: (0, at + i))],
            out_specs=[pl.BlockSpec((BLK, step * HW), lambda i, ln, ev, sh: (0, i))] * 2,
            scratch_shapes=[pltpu.VMEM((2 * BLK, step * HW), jnp.bfloat16)],
        ),
        out_shape=[jax.ShapeDtypeStruct((BLK, heads * HW), jnp.bfloat16)] * 2,
        compiler_params=pltpu.CompilerParams(vmem_limit_bytes=VMEM),
        cost_estimate=worth(heads * flops),
        name="parked_grads",
    )(lengths, evicted, quarters, *pieces, *[in_hbm(grad_out)] * 2, in_hbm(third))


def place_kernel(slots, firsts, flagged, lengths, evicted, flag, *refs):
    count = len(slots)
    pieces, (out, sems) = refs[:count], refs[-2:]
    plan = Plan(lengths, evicted)

    def store(n, slot):
        start = pl.multiple_of(slots[n](plan, slot) * BLK, BLK)
        return pltpu.make_async_copy(
            pieces[n].at[pl.ds(slot * BLK, BLK), :],
            out.at[pl.ds(start, BLK), pl.ds(firsts[n] * HW, pieces[n].shape[1])],
            sems.at[n, slot],
        )

    def begin(n):
        for slot in range(pieces[n].shape[0] // BLK):
            store(n, slot).start()

    def finish(n):
        for slot in range(pieces[n].shape[0] // BLK):
            store(n, slot).wait()

    for step in (begin, finish):
        for n in range(count):
            run = functools.partial(step, n)
            if flagged[n]:
                pl.when(flag[0] > 0)(run)
            else:
                run()


def place(lengths, evicted, flag, out, total, *items):
    pieces, slots, firsts, flagged = zip(*items)
    base = (lengths, evicted, flag, *pieces) + (() if out is None else (out,))
    smem, free = pl.BlockSpec(memory_space=pltpu.SMEM), pl.BlockSpec(memory_space=pl.ANY)
    count = len(items)
    return pl.pallas_call(
        functools.partial(place_kernel, slots, firsts, flagged),
        in_specs=[smem] * 3 + [free] * (len(base) - 3),
        out_specs=free,
        scratch_shapes=[pltpu.SemaphoreType.DMA((count, 2))],
        out_shape=jax.ShapeDtypeStruct(total, jnp.bfloat16),
        input_output_aliases={} if out is None else {3 + count: 0},
        compiler_params=pltpu.CompilerParams(vmem_limit_bytes=1 << 20),
        cost_estimate=worth(PLACE_COST),
        name="place_rows",
    )(*base)


def shards(kept_rows, parked_rows, grad_out, lengths, evicted):
    sections, peers = lax.axis_size("section"), lax.axis_size("tp")
    half = sections // 2
    ring = 2 * peers
    total = (grad_out.shape[0], kept_rows.shape[1])
    share = total[1]
    spot = 2 * lax.axis_index("tp") + lax.axis_index("section") // half

    def shifted(rows, hops):
        pairs = []
        for s in range(sections):
            for t in range(peers):
                to = (2 * t + s // half + hops) % ring
                pairs.append((s * peers + t, ((s + half) % sections) * peers + to // 2))
        return lax.ppermute(rows, ("section", "tp"), pairs)

    def passed_back(rows, within=sections):
        pairs = [(i, i // within * within + (i - 1) % within) for i in range(sections)]
        return lax.ppermute(rows, "section", pairs)

    def across_ends(rows):
        return lax.ppermute(rows, "section", [(half - 1, sections - 1), (sections - 1, half - 1)])

    last = (lax.rem(lax.axis_index("section"), half) == half - 1).astype(jnp.int32).reshape(1)

    def parked_slice(hops, first, heads):
        to = lax.rem(spot + hops + ring, ring) // 2
        return lax.dynamic_slice(
            parked_rows, (0, to * share + first * HW), (parked_rows.shape[0], heads * HW)
        )

    def parked_piece(hops, first, heads):
        return shifted(parked_slice(hops, first, heads), hops)

    def once(value, *done):
        return lax.optimization_barrier((value, *done))[0]

    quarters = jnp.stack([lax.rem(spot - hops + ring, ring) // 2 for hops in HOPS]).astype(jnp.int32)
    p1, p2 = PARKED_CHUNKS
    far, near = HOPS[:2], HOPS[2:]
    far_rows = [parked_slice(hops, 0, p1) for hops in far]
    z1 = [shifted(rows, hops) for rows, hops in zip(far_rows, far)]
    next_evicted = passed_back(once(evicted, *far_rows))
    both = [parked_piece(hops, 0, p1 + p2) for hops in near]
    z2 = [parked_piece(hops, p1, p2) for hops in far]
    early, third = kept_part(lengths, evicted, kept_rows, grad_out, 0, p1 + p2)
    x1 = passed_back(once(early, next_evicted), half)
    late1 = parked_part(lengths, evicted, quarters, z1 + both, grad_out, third, 0, p1, PARKED_COST)
    x2 = [passed_back(rows) for rows in late1]
    x1_ends = across_ends(once(x1, *late1))
    out = place(lengths, next_evicted, last, None, total, (x1, Plan.kept, 0, False))
    late2 = parked_part(
        once(lengths, *late1, out), evicted, quarters, z2 + both, grad_out, third, p1, p2, LATE_COST, p1
    )
    x3 = [passed_back(rows) for rows in late2]
    slots = (lambda plan, slot: plan.late(0), lambda plan, slot: plan.late(1))
    pieces = lambda rows, first: [(part, to, first, False) for part, to in zip(rows, slots)]
    out = place(lengths, next_evicted, last, out, total, *pieces(x2, 0))
    return place(lengths, next_evicted, last, out, total, (x1_ends, Plan.kept, 0, True), *pieces(x3, p1))


def solution(mesh):
    in_specs = (
        P("section", "tp"),
        P(("section", "tp"), None),
        P("section", "tp"),
        P(),
        P("section"),
    )
    out_specs = P("section", "tp")
    return jax.shard_map(shards, mesh=mesh, in_specs=in_specs, out_specs=out_specs, check_vma=False)
```
